256 devices in a mesh: row: 16 (over z, x_hi), col: 16 (over x_lo, y, core).
Axes of the slice: x: 4 (x_hi: 2, x_lo: 2; x = x_hi * 2 + x_lo), y: 4, z: 8, core: 2. Of those that a mesh axis runs over, the one named last changes fastest.
Arguments:
- acquired_tiles: bfloat16 [4, 262144, 1024], P(None, ('row', 'col')), may hold values from -24 to 24
- row_live: int32 [4, 262144], P(None, ('row', 'col')), may hold values from 0 to 1, as said below
- col_live: int32 [4, 262144], P(None, ('row', 'col')), may hold values 0 or 1
- row_order: int32 [16], replicated, may hold values from 0 to 15, as said below
- source_init: float32 [262144, 256], P(('row', 'col')), may hold values from -3 to 3
- receiver_init: float32 [262144, 256], P(('row', 'col')), may hold values from -3 to 3
Outputs:
- sources: float32 [262144, 256], P(('row', 'col'))
- receivers: float32 [262144, 256], P(('row', 'col'))
The draws below stay inside these ranges and needn't reach their ends.
Inputs may be any that keep to these rules, and one draw needn't show every extreme that they name: `row_live`: 1 where the source of that row is recorded in that stratum's tile; sources go missing singly and in whole aligned lines of 128 rows, and the share of missing lines differs from block to block. `row_order`: each number once.
All inputs are finite; a program needn't handle non-finite values. No bound on the sum of `col_live` on one device may be relied on, other than what follows from the above.
Results may differ from the reference program's by a relative error of at most 0.00096.
Values sent between devices are 32-bit elements; how exact they have to be, the bound alone decides.
No kernel may reach another device: no remote copies, remote signals or barrier semaphores. Data moves between devices by JAX's collectives and lax.ppermute only.
A program may use at most 128 MiB of HBM per device.

```python
import jax
import jax.numpy as jnp
from jax import lax

K = 256
BLOCK = 1024
BAND = 128
STRATA = 4
STEPS = 2
ORDER = 262144
N_ROW = 16
N_COL = 16
DEVICES = 256


def draw_row_live(key, part):
    seeded = jax.random.fold_in(key, 7)
    first_key, second_key = jax.random.split(seeded)
    band_total = ORDER // BAND
    owner_block = jnp.arange(band_total, dtype=jnp.int32) * BAND // BLOCK
    threshold = owner_block * 7 // DEVICES
    band_draw = jax.random.randint(first_key, (STRATA, band_total), 0, 10)
    band_live = (band_draw >= threshold[None, :]).astype(jnp.int32)
    single = (jax.random.randint(second_key, (STRATA, ORDER), 0, 5) > 0).astype(jnp.int32)
    return jnp.repeat(band_live, BAND, axis=1) * single


def draw_row_order(key, part):
    seeded = jax.random.fold_in(key, 17)
    perm_key, pick_key = jax.random.split(seeded)
    shuffled = jax.random.permutation(perm_key, N_ROW).astype(jnp.int32)
    chosen = jax.random.randint(pick_key, (), 0, N_ROW).astype(jnp.int32)
    wanted = (chosen + N_ROW - 1) % N_ROW
    positions = jnp.arange(N_ROW, dtype=jnp.int32)
    holder = jnp.sum(jnp.where(shuffled == wanted, positions, 0)).astype(jnp.int32)
    displaced = jnp.sum(jnp.where(positions == chosen, shuffled, 0)).astype(jnp.int32)
    result = jnp.where(positions == holder, displaced, shuffled)
    result = jnp.where(positions == chosen, wanted, result)
    return result.astype(jnp.int32)


def factor_draw(key, salt):
    seeded = jax.random.fold_in(key, salt)
    base_key = jax.random.fold_in(seeded, 0)
    values = 0.5 * jax.random.normal(base_key, (ORDER, K), jnp.float32)
    return jnp.clip(values, -3.0, 3.0)


def draw_source_init(key, part):
    return factor_draw(key, 11)


def draw_receiver_init(key, part):
    return factor_draw(key, 13)


def place_ends(drawn, rng, low, largest):
    index_at = [jax.random.randint(jax.random.fold_in(rng, axis), (), 0, length) for axis, length in enumerate(drawn.shape)]
    widest = drawn.shape.index(max(drawn.shape))
    neighbour = index_at[:widest] + [(index_at[widest] + 1) % drawn.shape[widest]] + index_at[widest + 1:]
    return drawn.at[tuple(index_at)].set(low).at[tuple(neighbour)].set(largest)


def steps_of(key, extent, pieces, smallest, top_value):
    loudness, own = 1.0, jax.random.fold_in(key, 6)
    for dim, parts in pieces:
        draws = jnp.exp(jax.random.uniform(jax.random.fold_in(own, dim), (parts,), jnp.float32, smallest / len(pieces), top_value / len(pieces)))
        loudness = loudness * jnp.repeat(draws, extent[dim] // parts).reshape([-1 if axis == dim else 1 for axis in range(len(extent))])
    return loudness


def scatter_about(own_key, shape, width, most, cuts=(), kind=jnp.bfloat16):
    level = steps_of(own_key, shape, cuts, -0.22, 0.18) if cuts else 1.0
    entries = jax.random.normal(own_key, shape, jnp.float32) * width * level
    return jnp.minimum(jnp.maximum(entries, -most), most).astype(kind)


def setup_inputs(seed: int = 0) -> dict:
    key_list = jax.random.split(jax.random.key(seed), 7)
    return {
        "acquired_tiles": scatter_about(key_list[0], (STRATA, ORDER, BLOCK), 4.0, 24.0, ((1, 256),)),
        "row_live": draw_row_live(jax.random.fold_in(key_list[6], 71), 0),
        "col_live": place_ends((jax.random.randint(key_list[2], (STRATA, ORDER), 0, 4) < 3).astype(jnp.int32), jax.random.fold_in(key_list[2], 1), 0, 1),
        "row_order": draw_row_order(jax.random.fold_in(key_list[6], 71), 0),
        "source_init": draw_source_init(jax.random.fold_in(key_list[6], 71), 0),
        "receiver_init": draw_receiver_init(jax.random.fold_in(key_list[6], 71), 0),
    }


def fit_block(src_block, rec_block, acquired, live_rows, live_cols):
    weights = live_rows.astype(jnp.float32)[:, None] * live_cols.astype(jnp.float32)[None, :]
    observed = acquired.astype(jnp.float32)
    step_size = 1.0 / (BLOCK + 2 * K)
    for iteration in range(STEPS):
        src_half = src_block.astype(jnp.bfloat16)
        rec_half = rec_block.astype(jnp.bfloat16)
        predicted = jnp.dot(src_half, rec_half.T, preferred_element_type=jnp.float32)
        misfit = (weights * (observed - predicted)).astype(jnp.bfloat16)
        grad_src = jnp.dot(misfit, rec_half, preferred_element_type=jnp.float32)
        grad_rec = jnp.dot(misfit.T, src_half, preferred_element_type=jnp.float32)
        src_block = src_block + step_size * grad_src
        rec_block = rec_block + step_size * grad_rec
    return src_block, rec_block


def reference(acquired_tiles, row_live, col_live, row_order, source_init, receiver_init):
    block_count = ORDER // BLOCK
    src_blocks = source_init.reshape(block_count, BLOCK, K)
    rec_blocks = receiver_init.reshape(block_count, BLOCK, K)
    for stratum in range(STRATA):
        slab_data = acquired_tiles[stratum].reshape(block_count, BLOCK, BLOCK)
        live_rows = row_live[stratum].reshape(block_count, BLOCK)
        live_cols = col_live[stratum].reshape(block_count, BLOCK)
        src_blocks, rec_blocks = lax.map(lambda packed: fit_block(*packed), (src_blocks, rec_blocks, slab_data, live_rows, live_cols))
        if stratum + 1 < STRATA:
            rec_blocks = jnp.roll(rec_blocks, 1, axis=0)
            if stratum == 1:
                rec_blocks = rec_blocks.reshape(N_ROW, N_COL, BLOCK, K)[row_order].reshape(block_count, BLOCK, K)
    return src_blocks.reshape(ORDER, K), rec_blocks.reshape(ORDER, K)
```

```python
import functools

import jax
import jax.numpy as jnp
from jax import lax
from jax.experimental import pallas as pl
from jax.experimental.pallas import tpu as pltpu
from jax.sharding import PartitionSpec as P

STEPS = 2
CHUNKS = 2
MIB = 1024 * 1024


def column_of(mask_row, width):
    tall = jnp.broadcast_to(mask_row.astype(jnp.float32), (8, mask_row.shape[1])).T
    return jnp.broadcast_to(tall[:, 0:1], (mask_row.shape[1], width))


def step_body(stratum, part, width, parts, joined, step_size, *refs):
    src_ref, tile_ref, rows_ref, cols_ref = refs[:4]
    rec_refs = refs[4 : 4 + joined]
    grad_ref = refs[4 + joined] if part else None
    sum_ref, new_rec_ref = refs[-2:]
    rank = src_ref.shape[1]
    window = slice(part * width, (part + 1) * width)
    live_rows = column_of(rows_ref[stratum : stratum + 1, :], rank)
    live_cols = column_of(cols_ref[stratum : stratum + 1, window], rank)
    src = src_ref[...]
    if joined > 1:
        rec = jnp.concatenate([ref[...] for ref in rec_refs], 0)
    elif rec_refs[0].shape[0] == width:
        rec = rec_refs[0][...]
    else:
        rec = rec_refs[0][window, :]
    src_half = src.astype(jnp.bfloat16)
    rec_half = rec.astype(jnp.bfloat16)
    src_live = (src * live_rows).astype(jnp.bfloat16)
    rec_live = (rec * live_cols).astype(jnp.bfloat16)
    predicted = lax.dot_general(
        src_half, rec_half, (((1,), (1,)), ((), ())), preferred_element_type=jnp.float32
    )
    misfit = (tile_ref[:, window].astype(jnp.float32) - predicted).astype(jnp.bfloat16)
    grad_src = jnp.dot(misfit, rec_live, preferred_element_type=jnp.float32)
    grad_rec = lax.dot_general(
        misfit, src_live, (((0,), (0,)), ((), ())), preferred_element_type=jnp.float32
    )
    new_rec_ref[...] = rec + (step_size * live_cols) * grad_rec
    if grad_ref is not None:
        grad_src = grad_src + grad_ref[...]
    if part == parts - 1:
        sum_ref[...] = src + (step_size * live_rows) * grad_src
    else:
        sum_ref[...] = grad_src


def step_part(stratum, part, parts, src, recs, tile, rows, cols, grad):
    size, rank = src.shape
    width = tile.shape[1] // parts
    step_size = 1.0 / (tile.shape[1] + 2 * rank)
    operands = [src, tile, rows, cols, *recs] + ([grad] if part else [])
    whole = pl.BlockSpec(memory_space=pltpu.VMEM)
    return pl.pallas_call(
        functools.partial(
            step_body, stratum, part, width, parts, len(recs), step_size
        ),
        out_shape=(
            jax.ShapeDtypeStruct((size, rank), jnp.float32),
            jax.ShapeDtypeStruct((width, rank), jnp.float32),
        ),
        in_specs=[whole] * len(operands),
        out_specs=(whole, whole),
        compiler_params=pltpu.CompilerParams(vmem_limit_bytes=28 * MIB),
        cost_estimate=pl.CostEstimate(
            flops=6 * size * width * rank,
            bytes_accessed=2 * size * width + 12 * size * rank,
            transcendentals=0,
        ),
    )(*operands)


def step(stratum, parts, src, recs, tile, rows, cols):
    grad, news = None, []
    for part in range(parts):
        mine = [recs[part]] if len(recs) == parts else recs
        grad, new = step_part(stratum, part, parts, src, mine, tile, rows, cols, grad)
        news.append(new)
    return grad, news


def pick_body(index_ref, pieces_ref, out_ref, sems):
    copies = [
        pltpu.make_async_copy(pieces_ref.at[index_ref[j]], out_ref.at[j], sems.at[j])
        for j in range(out_ref.shape[0])
    ]
    for copy in copies:
        copy.start()
    for copy in copies:
        copy.wait()


def pick(pieces, index):
    return pl.pallas_call(
        pick_body,
        out_shape=jax.ShapeDtypeStruct(pieces.shape, pieces.dtype),
        in_specs=[
            pl.BlockSpec(memory_space=pltpu.SMEM),
            pl.BlockSpec(memory_space=pl.ANY),
        ],
        out_specs=pl.BlockSpec(memory_space=pl.ANY),
        scratch_shapes=[pltpu.SemaphoreType.DMA((pieces.shape[0],))],
        cost_estimate=pl.CostEstimate(
            flops=0, bytes_accessed=2 * 4 * pieces.size, transcendentals=0
        ),
    )(index, pieces)


def onward(block, axes):
    count = lax.axis_size(axes)
    return lax.ppermute(block, axes, [(i, (i + 1) % count) for i in range(count)])


def reassign(rec_block, row_order):
    rows = lax.axis_size("row")
    size, rank = rec_block.shape
    wraps = (lax.axis_index("col") == lax.axis_size("col") - 1).astype(jnp.int32)
    index = (row_order + (rows - wraps)) % rows
    pieces = lax.all_to_all(
        rec_block.reshape(rows, size // rows, rank), "row", 0, 0, tiled=True
    )
    pieces = lax.all_to_all(pick(pieces, index), "row", 0, 0, tiled=True)
    return pieces.reshape(size, rank)


def later(array, before):
    return lax.optimization_barrier((array, before))[0]


def local(acquired_tiles, row_live, col_live, row_order, source_init, receiver_init):
    strata = acquired_tiles.shape[0]
    part = receiver_init.shape[0] // CHUNKS
    src, recs = source_init, [receiver_init]
    for stratum in range(strata):
        ahead = stratum + 1 < strata and stratum != 1
        tile = (acquired_tiles if stratum == 0 else later(acquired_tiles, src))[stratum]
        src, recs = step(stratum, len(recs), src, recs, tile, row_live, col_live)
        src, recs = step(
            stratum, CHUNKS if ahead else 1, src, recs, tile, row_live, col_live
        )
        if ahead:
            recs = [onward(rec, ("row", "col")) for rec in recs]
        elif stratum == 1:
            whole = reassign(recs[0], row_order)
            recs = [
                onward(whole[i * part : (i + 1) * part], "col") for i in range(CHUNKS)
            ]
    return src, recs[0]


def solution(mesh):
    placed = (
        P(None, ("row", "col"), None),
        P(None, ("row", "col")),
        P(None, ("row", "col")),
        P(),
        P(("row", "col"), None),
        P(("row", "col"), None),
    )
    return jax.shard_map(
        local,
        mesh=mesh,
        in_specs=placed,
        out_specs=(P(("row", "col"), None), P(("row", "col"), None)),
        check_vma=False,
    )
```

```python
import functools

import jax
import jax.numpy as jnp
from jax import lax
from jax.experimental import pallas as pl
from jax.experimental.pallas import tpu as pltpu
from jax.sharding import PartitionSpec as P

PARTS = (1, 1)
MIB = 1024 * 1024


def column_of(mask_row, width):
    tall = jnp.broadcast_to(mask_row.astype(jnp.float32), (8, mask_row.shape[1])).T
    return jnp.broadcast_to(tall[:, 0:1], (mask_row.shape[1], width))


def step_body(stratum, start, stop, ends, whole, step_size, *refs):
    src_ref, tile_ref, rows_ref, cols_ref = refs[:4]
    rec_refs = refs[4 : len(refs) - 2 - (start > 0)]
    grad_ref = refs[-3] if start else None
    sum_ref, new_rec_ref = refs[-2:]
    rank = src_ref.shape[1]
    window = slice(start, stop)
    live_rows = column_of(rows_ref[stratum : stratum + 1, :], rank)
    live_cols = column_of(cols_ref[stratum : stratum + 1, window], rank)
    src = src_ref[...]
    if whole:
        rec = rec_refs[0][window, :]
    else:
        rec = jnp.concatenate([ref[...] for ref in rec_refs], 0)
    src_half = src.astype(jnp.bfloat16)
    rec_half = rec.astype(jnp.bfloat16)
    src_live = (src * live_rows).astype(jnp.bfloat16)
    rec_live = (rec * live_cols).astype(jnp.bfloat16)
    predicted = lax.dot_general(
        src_half, rec_half, (((1,), (1,)), ((), ())), preferred_element_type=jnp.float32
    )
    misfit = (tile_ref[:, window].astype(jnp.float32) - predicted).astype(jnp.bfloat16)
    grad_src = jnp.dot(misfit, rec_live, preferred_element_type=jnp.float32)
    grad_rec = lax.dot_general(
        misfit, src_live, (((0,), (0,)), ((), ())), preferred_element_type=jnp.float32
    )
    new_rec_ref[...] = rec + (step_size * live_cols) * grad_rec
    if grad_ref is not None:
        grad_src = grad_src + grad_ref[...]
    if ends:
        sum_ref[...] = src + (step_size * live_rows) * grad_src
    else:
        sum_ref[...] = grad_src


def spans(size):
    unit = size // sum(PARTS)
    ends = [unit * sum(PARTS[: i + 1]) for i in range(len(PARTS))]
    return list(zip([0] + ends[:-1], ends))


def step_part(stratum, start, stop, src, recs, tile, rows, cols, grad):
    size, rank = src.shape
    width = stop - start
    step_size = 1.0 / (size + 2 * rank)
    operands = [src, tile, rows, cols, *recs] + ([grad] if start else [])
    whole = recs[0].shape[0] > width
    vmem = pl.BlockSpec(memory_space=pltpu.VMEM)
    return pl.pallas_call(
        functools.partial(
            step_body, stratum, start, stop, stop == size, whole, step_size
        ),
        out_shape=(
            jax.ShapeDtypeStruct((size, rank), jnp.float32),
            jax.ShapeDtypeStruct((width, rank), jnp.float32),
        ),
        in_specs=[vmem] * len(operands),
        out_specs=(vmem, vmem),
        compiler_params=pltpu.CompilerParams(vmem_limit_bytes=28 * MIB),
        cost_estimate=pl.CostEstimate(
            flops=6 * size * width * rank,
            bytes_accessed=2 * size * width + 12 * size * rank,
            transcendentals=0,
        ),
    )(*operands)


def step(stratum, src, recs, tile, *live):
    grad, news = None, []
    for part, (start, stop) in enumerate(spans(tile.shape[1])):
        mine = recs[part : part + 1] if len(recs) > 1 else recs
        grad, new = step_part(stratum, start, stop, src, mine, tile, *live, grad)
        news.append(new)
    return grad, news


def step_at_once(stratum, src, recs, tile, *live):
    return step_part(stratum, 0, tile.shape[1], src, recs, tile, *live, None)


def pick_body(index_ref, pieces_ref, out_ref):
    for j in range(out_ref.shape[0]):
        out_ref[j] = pieces_ref[index_ref[j]]


def pick(pieces, index):
    return pl.pallas_call(
        pick_body,
        out_shape=jax.ShapeDtypeStruct(pieces.shape, pieces.dtype),
        in_specs=[
            pl.BlockSpec(memory_space=pltpu.SMEM),
            pl.BlockSpec(memory_space=pltpu.VMEM),
        ],
        out_specs=pl.BlockSpec(memory_space=pltpu.VMEM),
        compiler_params=pltpu.CompilerParams(vmem_limit_bytes=8 * MIB),
        cost_estimate=pl.CostEstimate(
            flops=0, bytes_accessed=2 * 4 * pieces.size, transcendentals=0
        ),
    )(index, pieces)


def onward(block, axes):
    count = lax.axis_size(axes)
    return lax.ppermute(block, axes, [(i, (i + 1) % count) for i in range(count)])


def reassign(block, row_order):
    rows = lax.axis_size("row")
    size, rank = block.shape
    wraps = (lax.axis_index("col") == lax.axis_size("col") - 1).astype(jnp.int32)
    index = (row_order + (rows - wraps)) % rows
    pieces = block.reshape(rows, size // rows, rank)
    pieces = lax.all_to_all(pieces, "row", 0, 0, tiled=True)
    pieces = lax.all_to_all(pick(pieces, index), "row", 0, 0, tiled=True)
    whole = pieces.reshape(size, rank)
    return [onward(whole[start:stop], "col") for start, stop in spans(size)]


def later(array, before):
    return lax.optimization_barrier((array, before))[0]


def local(acquired_tiles, row_live, col_live, row_order, source_init, receiver_init):
    live = (row_live, col_live)
    tile = acquired_tiles[0]
    src, rec = step_at_once(0, source_init, [receiver_init], tile, *live)
    src, recs = step(0, src, [rec], tile, *live)
    recs = [onward(rec, ("row", "col")) for rec in recs]

    tile = later(acquired_tiles, src)[1]
    src, recs = step(1, src, recs, tile, *live)
    src, rec = step_at_once(1, src, recs, tile, *live)
    recs = reassign(rec, row_order)

    tile = later(acquired_tiles, rec)[2]
    src, recs = step(2, src, recs, tile, *live)
    src, recs = step(2, src, recs, tile, *live)
    recs = [onward(rec, ("row", "col")) for rec in recs]

    tile = later(acquired_tiles, src)[3]
    src, recs = step(3, src, recs, tile, *live)
    return step_at_once(3, src, recs, tile, *live)


def solution(mesh):
    placed = (
        P(None, ("row", "col"), None),
        P(None, ("row", "col")),
        P(None, ("row", "col")),
        P(),
        P(("row", "col"), None),
        P(("row", "col"), None),
    )
    return jax.shard_map(
        local,
        mesh=mesh,
        in_specs=placed,
        out_specs=(P(("row", "col"), None), P(("row", "col"), None)),
        check_vma=False,
    )
```

```python
import functools

import jax
import jax.numpy as jnp
from jax import lax
from jax.experimental import pallas as pl
from jax.experimental.pallas import tpu as pltpu
from jax.sharding import PartitionSpec as P

PARTS = (1, 1)
MIB = 1024 * 1024


def column_of(mask_row, width):
    tall = jnp.broadcast_to(mask_row.astype(jnp.float32), (8, mask_row.shape[1])).T
    return jnp.broadcast_to(tall[:, 0:1], (mask_row.shape[1], width))


def step_body(stratum, start, stop, ends, whole, step_size, *refs):
    src_ref, tile_ref, rows_ref, cols_ref = refs[:4]
    rec_refs = refs[4 : len(refs) - 3 - (start > 0)]
    grad_ref = refs[-4] if start else None
    sum_ref, new_rec_ref, misfit_ref = refs[-3:]
    rank = src_ref.shape[1]
    window = slice(start, stop)
    live_rows = column_of(rows_ref[stratum : stratum + 1, :], rank)
    live_cols = column_of(cols_ref[stratum : stratum + 1, window], rank)
    src = src_ref[...]
    if whole:
        rec = rec_refs[0][window, :]
    else:
        rec = jnp.concatenate([ref[...] for ref in rec_refs], 0)
    src_half = src.astype(jnp.bfloat16)
    rec_half = rec.astype(jnp.bfloat16)
    src_live = (src * live_rows).astype(jnp.bfloat16)
    rec_live = (rec * live_cols).astype(jnp.bfloat16)
    size = src.shape[0]
    high = size // 2 if stop - start == size else size
    for top in range(0, size, high):
        band = slice(top, top + high)
        predicted = lax.dot_general(
            src_half[band, :],
            rec_half,
            (((1,), (1,)), ((), ())),
            preferred_element_type=jnp.float32,
        )
        misfit = tile_ref[band, window].astype(jnp.float32) - predicted
        misfit = misfit.astype(jnp.bfloat16)
        if high < size:
            misfit_ref[band, :] = misfit
        grad_src = jnp.dot(misfit, rec_live, preferred_element_type=jnp.float32)
        if grad_ref is not None:
            grad_src = grad_src + grad_ref[band, :]
        if ends:
            grad_src = src[band, :] + (step_size * live_rows[band, :]) * grad_src
        sum_ref[band, :] = grad_src
    grad_rec = lax.dot_general(
        misfit_ref[...] if high < size else misfit,
        src_live,
        (((0,), (0,)), ((), ())),
        preferred_element_type=jnp.float32,
    )
    new_rec_ref[...] = rec + (step_size * live_cols) * grad_rec


def spans(size):
    unit = size // sum(PARTS)
    ends = [unit * sum(PARTS[: i + 1]) for i in range(len(PARTS))]
    return list(zip([0] + ends[:-1], ends))


def step_part(stratum, start, stop, src, recs, tile, rows, cols, grad):
    size, rank = src.shape
    width = stop - start
    step_size = 1.0 / (size + 2 * rank)
    operands = [src, tile, rows, cols, *recs] + ([grad] if start else [])
    whole = recs[0].shape[0] > width
    vmem = pl.BlockSpec(memory_space=pltpu.VMEM)
    return pl.pallas_call(
        functools.partial(
            step_body, stratum, start, stop, stop == size, whole, step_size
        ),
        out_shape=(
            jax.ShapeDtypeStruct((size, rank), jnp.float32),
            jax.ShapeDtypeStruct((width, rank), jnp.float32),
        ),
        in_specs=[vmem] * len(operands),
        out_specs=(vmem, vmem),
        scratch_shapes=[pltpu.VMEM((size, width), jnp.bfloat16)],
        compiler_params=pltpu.CompilerParams(vmem_limit_bytes=28 * MIB),
        cost_estimate=pl.CostEstimate(
            flops=6 * size * width * rank,
            bytes_accessed=2 * size * width + 12 * size * rank,
            transcendentals=0,
        ),
    )(*operands)


def step(stratum, src, recs, tile, *live):
    grad, news = None, []
    for part, (start, stop) in enumerate(spans(tile.shape[1])):
        mine = recs[part : part + 1] if len(recs) > 1 else recs
        grad, new = step_part(stratum, start, stop, src, mine, tile, *live, grad)
        news.append(new)
    return grad, news


def step_at_once(stratum, src, recs, tile, *live):
    return step_part(stratum, 0, tile.shape[1], src, recs, tile, *live, None)


def pick_body(index_ref, pieces_ref, out_ref):
    for j in range(out_ref.shape[0]):
        out_ref[j] = pieces_ref[index_ref[j]]


def pick(pieces, index):
    return pl.pallas_call(
        pick_body,
        out_shape=jax.ShapeDtypeStruct(pieces.shape, pieces.dtype),
        in_specs=[
            pl.BlockSpec(memory_space=pltpu.SMEM),
            pl.BlockSpec(memory_space=pltpu.VMEM),
        ],
        out_specs=pl.BlockSpec(memory_space=pltpu.VMEM),
        compiler_params=pltpu.CompilerParams(vmem_limit_bytes=8 * MIB),
        cost_estimate=pl.CostEstimate(
            flops=0, bytes_accessed=2 * 4 * pieces.size, transcendentals=0
        ),
    )(index, pieces)


def onward(block, axes):
    count = lax.axis_size(axes)
    return lax.ppermute(block, axes, [(i, (i + 1) % count) for i in range(count)])


def reassign(block, row_order):
    rows = lax.axis_size("row")
    size, rank = block.shape
    wraps = (lax.axis_index("col") == lax.axis_size("col") - 1).astype(jnp.int32)
    index = (row_order + (rows - wraps)) % rows
    pieces = block.reshape(rows, size // rows, rank)
    pieces = lax.all_to_all(pieces, "row", 0, 0, tiled=True)
    pieces = lax.all_to_all(pick(pieces, index), "row", 0, 0, tiled=True)
    whole = pieces.reshape(size, rank)
    return [onward(whole[start:stop], "col") for start, stop in spans(size)]


def later(array, before):
    return lax.optimization_barrier((array, before))[0]


def local(acquired_tiles, row_live, col_live, row_order, source_init, receiver_init):
    live = (row_live, col_live)
    tile = acquired_tiles[0]
    src, rec = step_at_once(0, source_init, [receiver_init], tile, *live)
    src, recs = step(0, src, [rec], tile, *live)
    recs = [onward(rec, ("row", "col")) for rec in recs]

    tile = later(acquired_tiles, src)[1]
    src, recs = step(1, src, recs, tile, *live)
    src, rec = step_at_once(1, src, recs, tile, *live)
    recs = reassign(rec, row_order)

    tile = later(acquired_tiles, rec)[2]
    src, recs = step(2, src, recs, tile, *live)
    src, recs = step(2, src, recs, tile, *live)
    recs = [onward(rec, ("row", "col")) for rec in recs]

    tile = later(acquired_tiles, src)[3]
    src, recs = step(3, src, recs, tile, *live)
    return step_at_once(3, src, recs, tile, *live)


def solution(mesh):
    placed = (
        P(None, ("row", "col"), None),
        P(None, ("row", "col")),
        P(None, ("row", "col")),
        P(),
        P(("row", "col"), None),
        P(("row", "col"), None),
    )
    return jax.shard_map(
        local,
        mesh=mesh,
        in_specs=placed,
        out_specs=(P(("row", "col"), None), P(("row", "col"), None)),
        check_vma=False,
    )
```
